256 devices in a mesh: dp: 64 (over y_hi, z, x), factor: 4 (over y_lo, core).
Axes of the slice: x: 4, y: 4 (y_hi: 2, y_lo: 2; y = y_hi * 2 + y_lo), z: 8, core: 2. Of those that a mesh axis runs over, the one named last changes fastest.
Arguments:
- acts: bfloat16 [49152, 4096], P('dp', 'factor'), may hold values from -400 to 400
Outputs:
- act_factor: float32 [2, 4096, 1024], P(None, ('factor', 'dp'))
The draws below stay inside these ranges and needn't reach their ends.
All inputs are finite; a program needn't handle non-finite values.
Results may differ from the reference program's by a relative error of at most 0.0003.
Values may be sent and summed in bfloat16 or wider, within the bound.
No kernel may reach another device: no remote copies, remote signals or barrier semaphores. Data moves between devices by JAX's collectives and lax.ppermute only.
A program may use at most 64 MiB of HBM per device.

```python
import jax
import jax.numpy as jnp
from jax import lax

D = 4096
REACH = 2
TOKENS = 49152
PANELS = 4
PANEL = 1024


def scaled_field(key, rows, cols, spread):
    key_base, key_row, key_col = jax.random.split(key, 3)
    base = jax.random.normal(key_base, (rows, cols), jnp.float32)
    row_scale = jnp.exp(jax.random.uniform(key_row, (rows, 1), jnp.float32, -spread, spread))
    col_scale = jnp.exp(jax.random.uniform(key_col, (1, cols), jnp.float32, -spread, spread))
    return 0.5 * row_scale * col_scale * base


def draw_acts(key, part):
    key = jax.random.fold_in(key, 11)
    return scaled_field(key, TOKENS, D, 1.15).astype(jnp.bfloat16)


def setup_inputs(seed: int = 0) -> dict:
    key_of = jax.random.split(jax.random.key(seed), 2)
    acts = draw_acts(jax.random.fold_in(key_of[1], 71), 0)
    return dict(acts=acts)


def factor_blocks(values):
    wide = values.astype(jnp.float32)
    blocks = []
    for step in range(REACH):
        rows = []
        for index in range(PANELS):
            own = wide[:, index * PANEL:(index + 1) * PANEL]
            other_index = (index + step) % PANELS
            other = wide[:, other_index * PANEL:(other_index + 1) * PANEL]
            rows.append(jnp.dot(own.T, other, precision=lax.Precision.HIGHEST, preferred_element_type=jnp.float32))
        blocks.append(jnp.concatenate(rows, axis=0))
    block_sums = jnp.stack(blocks)
    return block_sums / TOKENS


def reference(acts):
    return factor_blocks(acts)
```

```python
import functools

import jax
import jax.numpy as jnp
from jax import lax
from jax.experimental import pallas as pl
from jax.experimental.pallas import tpu as pltpu
from jax.sharding import Mesh, PartitionSpec as P

SIZES = {"yh": 2, "z": 8, "x": 4, "yl": 2, "core": 2}
DP = ("yh", "z", "x")
FACTOR = ("yl", "core")
YZ = ("yh", "z")
NX, NYZ = SIZES["x"], SIZES["yh"] * SIZES["z"]
NF = SIZES["yl"] * SIZES["core"]
TOP = 15.0
VMEM = 48 * 1024 * 1024


def share(index, count):
    return 1.0 - 0.5 * jnp.float32(index) / count


def lifted(power, factor):
    return jnp.max(jnp.exp2(jnp.full((8, 128), TOP - power))) * factor


def lowered(power, factor):
    return jnp.max(jnp.exp2(jnp.full((8, 128), power - TOP))) / factor


def gram_kernel(own_ref, partner_ref, out_ref):
    tokens, panel = own_ref.shape
    count = panel // NX
    rows = panel // (NX * NYZ)
    here = lax.axis_index("x")
    largest = lambda ref: jnp.max(jnp.abs(ref[...]).astype(jnp.float32))
    bound = tokens * (largest(own_ref) + 1e-15) * (largest(partner_ref) + 1e-15)
    power = jnp.max(jnp.ceil(jnp.log2(jnp.full((8, 128), bound))))
    up = lifted(power, share(here, NX))
    for by in range(NX):
        out_ref[by, count:, :] = jnp.full((8, panel), power)
    chunk = 256
    for c in range(panel // chunk):
        product = lax.dot_general(
            own_ref[:, c * chunk : (c + 1) * chunk], partner_ref[...], (((0,), (0,)), ((), ())),
            preferred_element_type=jnp.float32,
        ) * up
        for n in range(chunk // rows):
            yz, x = divmod(c * (chunk // rows) + n, NX)
            by = lax.rem(x - here + NX, NX)
            out_ref[by, yz * rows : (yz + 1) * rows, :] = product[n * rows : (n + 1) * rows]


def gram(own, partner):
    tokens, panel = own.shape
    return pl.pallas_call(
        gram_kernel,
        out_shape=jax.ShapeDtypeStruct((NX, panel // NX + 8, panel), jnp.float32),
        in_specs=[pl.BlockSpec(memory_space=pltpu.VMEM)] * 2,
        out_specs=pl.BlockSpec(memory_space=pltpu.VMEM),
        compiler_params=pltpu.CompilerParams(vmem_limit_bytes=VMEM),
        cost_estimate=pl.CostEstimate(flops=2 * tokens * panel * panel, bytes_accessed=8 << 20, transcendentals=0),
        name="gram",
    )(own, partner)


def x_sum_kernel(own_ref, *refs):
    others, out_ref = refs[:-1], refs[-1]
    count, panel = own_ref.shape[1] - 8, own_ref.shape[2]
    here = lax.axis_index("x")
    power_of = lambda block: jnp.max(block[count:, :128])
    blocks = [own_ref.at[0], *others]
    powers = [power_of(block) for block in blocks]
    power = functools.reduce(jnp.maximum, powers) + 2.0
    iyz = lax.axis_index("yh") * SIZES["z"] + lax.axis_index("z")
    up = lifted(power, share(iyz, NYZ))
    weights = [lowered(p, share(lax.rem(here - by + NX, NX), NX)) * up for by, p in enumerate(powers)]
    rows = count // NYZ
    for n in range(NYZ):
        part = pl.ds(n * rows, rows)
        out_ref[n, :, :panel] = functools.reduce(
            lambda a, b: a + b, [block[part, :] * w for block, w in zip(blocks, weights)]
        )
        out_ref[n, :, panel:] = jnp.full((rows, 128), power)


def x_sum(own, others):
    _, count, panel = own.shape
    rows = (count - 8) // NYZ
    return pl.pallas_call(
        x_sum_kernel,
        grid=(1,),
        out_shape=jax.ShapeDtypeStruct((NYZ, rows, panel + 128), jnp.float32),
        in_specs=[pl.BlockSpec((1, count, panel), lambda i: (0, 0, 0))]
        + [pl.BlockSpec((count, panel), lambda i: (0, 0))] * (NX - 1),
        out_specs=pl.BlockSpec((NYZ, rows, panel + 128), lambda i: (0, 0, 0)),
        compiler_params=pltpu.CompilerParams(vmem_limit_bytes=VMEM),
        cost_estimate=pl.CostEstimate(flops=8 << 18, bytes_accessed=5 << 20, transcendentals=0),
        name="x_sum",
    )(own, *others)


def yz_sum_kernel(scale, got_ref, out_ref):
    panel = out_ref.shape[2]
    for k in range(2):
        weights = [
            jnp.exp2(got_ref[s, k, :, panel:] - TOP) * (scale / float(1.0 - 0.5 * s / NYZ)) for s in range(NYZ)
        ]
        for j in range(panel // 128):
            part = slice(j * 128, (j + 1) * 128)
            out_ref[k, :, part] = functools.reduce(
                lambda a, b: a + b, [got_ref[s, k, :, part] * w for s, w in enumerate(weights)]
            )


def yz_sum(got, scale):
    _, _, rows, wide = got.shape
    return pl.pallas_call(
        functools.partial(yz_sum_kernel, scale),
        out_shape=jax.ShapeDtypeStruct((2, rows, wide - 128), jnp.float32),
        in_specs=[pl.BlockSpec(memory_space=pltpu.VMEM)],
        out_specs=pl.BlockSpec(memory_space=pltpu.VMEM),
        compiler_params=pltpu.CompilerParams(vmem_limit_bytes=VMEM),
        cost_estimate=pl.CostEstimate(flops=1 << 20, bytes_accessed=3 << 20, transcendentals=0),
        name="yz_sum",
    )(got)


def per_device(acts):
    tokens, panel = acts.shape
    scale = 1.0 / (tokens * NX * NYZ)
    partner = lax.ppermute(acts, FACTOR, [(i, (i - 1) % NF) for i in range(NF)])

    def over_x(other):
        scaled = gram(acts, other)
        got = [None] * (NX - 1)
        for by in (2, 1, 3):
            pairs = [(i, (i + by) % NX) for i in range(NX)]
            got[by - 1] = lax.ppermute(scaled[by].astype(jnp.float16), "x", pairs).astype(jnp.float32)
        return x_sum(scaled, got)

    both = jnp.stack([over_x(acts), over_x(partner)], axis=1).astype(jnp.float16)
    got = lax.all_to_all(both, YZ, 0, 0, tiled=True)
    return yz_sum(got.astype(jnp.float32), scale)


def solution(mesh):
    fine = Mesh(mesh.devices.reshape(tuple(SIZES.values())), tuple(SIZES))
    return jax.shard_map(
        per_device,
        mesh=fine,
        in_specs=(P(DP, FACTOR),),
        out_specs=P(None, FACTOR + DP, None),
        check_vma=False,
    )
```

```python
import functools

import jax
import jax.numpy as jnp
from jax import lax
from jax.experimental import pallas as pl
from jax.experimental.pallas import tpu as pltpu
from jax.sharding import Mesh, PartitionSpec as P

SIZES = {"yh": 2, "z": 8, "x": 4, "yl": 2, "core": 2}
DP = ("yh", "z", "x")
FACTOR = ("yl", "core")
NX, NY, NZ = SIZES["x"], SIZES["yh"], SIZES["z"]
NF = SIZES["yl"] * SIZES["core"]
TOP = 15.0
VMEM = 48 * 1024 * 1024
CHUNK = 256


def share(index, count):
    return 1.0 - 0.5 * jnp.float32(index) / count


def lifted(power, factor):
    return jnp.max(jnp.exp2(jnp.full((8, 128), TOP - power))) * factor


def lowered(power, factor):
    return jnp.max(jnp.exp2(jnp.full((8, 128), power - TOP))) / factor


def ahead(axis, by):
    count = SIZES[axis]
    return lax.rem(lax.axis_index(axis) + by + count, count)


def sum_of(terms):
    return functools.reduce(lambda a, b: a + b, terms)


def rows_of(start, count):
    return pl.ds(pl.multiple_of(start, 16), count)


def senders(axis, blocks, growth):
    powers = [jnp.max(block[block.shape[0] - 8 :, :128]) for block in blocks]
    weights = [lowered(p, share(ahead(axis, -by), SIZES[axis])) for by, p in enumerate(powers)]
    return weights, functools.reduce(jnp.maximum, powers) + growth


def products(own_ref, partner_ref, visit):
    tokens, panel = own_ref.shape
    rows = panel // (NX * NY * NZ)
    largest = lambda ref: jnp.max(jnp.abs(ref[...]).astype(jnp.float32))
    bound = tokens * (largest(own_ref) + 1e-15) * (largest(partner_ref) + 1e-15)
    power = jnp.max(jnp.ceil(jnp.log2(jnp.full((8, 128), bound))))
    up = lifted(power, 1.0)
    for c in range(panel // CHUNK):
        product = lax.dot_general(
            own_ref[:, c * CHUNK : (c + 1) * CHUNK], partner_ref[...], (((0,), (0,)), ((), ())),
            preferred_element_type=jnp.float32,
        ) * up
        for n in range(CHUNK // rows):
            yz, x = divmod(c * (CHUNK // rows) + n, NX)
            visit(x, yz // NZ, yz % NZ, product[n * rows : (n + 1) * rows])
    return power


def diagonal_kernel(own_ref, partner_ref, out_ref):
    factor = share(lax.axis_index("x"), NX)

    def visit(x, y, z, value):
        rows = value.shape[0]
        to_x = lax.rem(x - lax.axis_index("x") + NX, NX)
        out_ref[to_x, rows_of((y * NZ + z) * rows, rows), :] = value * factor

    power = products(own_ref, partner_ref, visit)
    out_ref[:, out_ref.shape[1] - 8 :, :] = jnp.full((NX, 8, out_ref.shape[2]), power)


def beside_kernel(own_ref, partner_ref, left_ref, right_ref):
    half = left_ref.shape[2]
    by_y, by_x = share(lax.axis_index("yh"), NY), share(lax.axis_index("x"), NX)

    def visit(x, y, z, value):
        rows = value.shape[0]
        to_x = lax.rem(x - lax.axis_index("x") + NX, NX)
        to_y = lax.rem(y - lax.axis_index("yh") + NY, NY)
        left_ref[to_y, rows_of((to_x * NZ + z) * rows, rows), :] = value[:, :half] * by_y
        right_ref[to_x, rows_of((y * NZ + z) * rows, rows), :] = value[:, half:] * by_x

    power = products(own_ref, partner_ref, visit)
    left_ref[:, left_ref.shape[1] - 8 :, :] = jnp.full((NY, 8, half), power)
    right_ref[:, right_ref.shape[1] - 8 :, :] = jnp.full((NX, 8, half), power)


def x_to_y_kernel(own_ref, *refs):
    out_ref = refs[-1]
    blocks = [own_ref.at[0], *refs[:-1]]
    weights, power = senders("x", blocks, 2.0)
    up = lifted(power, share(lax.axis_index("yh"), NY))
    count = out_ref.shape[1] - 8
    for by in range(NY):
        part = rows_of(ahead("yh", by) * count, count)
        out_ref[by, :count, :] = sum_of([block[part, :] * (w * up) for block, w in zip(blocks, weights)])
    out_ref[:, count:, :] = jnp.full((NY, 8, out_ref.shape[2]), power)


def y_to_x_kernel(own_ref, got_ref, out_ref):
    blocks = [own_ref.at[0], got_ref]
    weights, power = senders("yh", blocks, 1.0)
    up = lifted(power, share(lax.axis_index("x"), NX))
    count = out_ref.shape[1] - 8
    for by in range(NX):
        part = pl.ds(by * count, count)
        out_ref[by, :count, :] = sum_of([block[part, :] * (w * up) for block, w in zip(blocks, weights)])
    out_ref[:, count:, :] = jnp.full((NX, 8, out_ref.shape[2]), power)


def to_z_kernel(*refs):
    first, right, left, out_ref = refs[:NY], refs[NY : 2 * NY], refs[2 * NY : -1], refs[-1]
    first, right, left = ([group[0].at[0], *group[1:]] for group in (first, right, left))
    w_first, p_first = senders("yh", first, 1.0)
    w_right, p_right = senders("yh", right, 1.0)
    w_left, p_left = senders("x", left, 2.0)
    power = jnp.maximum(p_first, jnp.maximum(p_right, p_left))
    up = lifted(power, share(lax.axis_index("z"), NZ))
    _, _, rows, wide = out_ref.shape
    panel = wide - 128
    half = panel // 2
    for z in range(NZ):
        part = pl.ds(z * rows, rows)
        total = lambda blocks, weights: sum_of([block[part, :] * (w * up) for block, w in zip(blocks, weights)])
        out_ref[z, 0, :, :panel] = total(first, w_first)
        out_ref[z, 1, :, :half] = total(left, w_left)
        out_ref[z, 1, :, half:panel] = total(right, w_right)
    out_ref[:, :, :, panel:] = jnp.full((NZ, 2, rows, 128), power)


def z_sum_kernel(scale, got_ref, out_ref):
    panel = out_ref.shape[2]
    for k in range(2):
        weights = [jnp.exp2(got_ref[s, k, :, panel:] - TOP) * (scale / float(1.0 - 0.5 * s / NZ)) for s in range(NZ)]
        for j in range(panel // 128):
            part = slice(j * 128, (j + 1) * 128)
            out_ref[k, :, part] = sum_of([got_ref[s, k, :, part] * w for s, w in enumerate(weights)])


def call(kernel, name, outs, *operands, flops=0):
    whole = lambda shape: pl.BlockSpec(shape, lambda i: (0,) * len(shape))
    arrays = [o[0] if isinstance(o, tuple) else o for o in operands]
    specs = [whole((1, *o[0].shape[1:]) if isinstance(o, tuple) else o.shape) for o in operands]
    out_shape = [jax.ShapeDtypeStruct(shape, jnp.float32) for shape in outs]
    moved = sum(a.size * a.dtype.itemsize for a in arrays) + sum(4 * s.size for s in out_shape)
    result = pl.pallas_call(
        kernel,
        grid=(1,),
        out_shape=out_shape,
        in_specs=specs,
        out_specs=[whole(s.shape) for s in out_shape],
        compiler_params=pltpu.CompilerParams(vmem_limit_bytes=VMEM),
        cost_estimate=pl.CostEstimate(flops=flops, bytes_accessed=moved, transcendentals=0),
        name=name,
    )(*arrays)
    return result if len(outs) > 1 else result[0]


def passed(value, axis, by):
    count = lax.axis_size(axis)
    return lax.ppermute(value, axis, [(i, (i + by) % count) for i in range(count)])


def per_device(acts):
    tokens, panel = acts.shape
    rows = panel // (NX * NY * NZ)
    half = panel // 2
    scale = 1.0 / (tokens * NX * NY * NZ)
    flops = 2 * tokens * panel * panel
    short = lambda value: value.astype(jnp.float16)
    long = lambda value: value.astype(jnp.float32)

    partner = passed(acts, FACTOR, NF - 1)

    first = call(diagonal_kernel, "diagonal", [(NX, NY * NZ * rows + 8, panel)], acts, acts, flops=flops)
    got_first = [passed(short(first[by]), "x", by) for by in range(1, NX)]

    left, right = call(
        beside_kernel, "beside", [(NY, NX * NZ * rows + 8, half), (NX, NY * NZ * rows + 8, half)], acts, partner,
        flops=flops,
    )
    left_sent, right_sent = short(left[1]), [short(right[by]) for by in range(1, NX)]
    got_left = passed(left_sent, "yh", 1)
    got_right = [passed(right_sent[by - 1], "x", by) for by in range(1, NX)]

    ahead_of = [long(jnp.concatenate([s, left_sent[: s.shape[0]]], axis=1)) for s in right_sent]
    got_first = [long(g) + 0.0 * s for g, s in zip(got_first, ahead_of)]

    lines = NZ * rows + 8
    first = call(x_to_y_kernel, "first_x", [(NY, lines, panel)], (first, 0), *got_first)
    got_first = passed(short(first[1]), "yh", 1)
    left = call(y_to_x_kernel, "left_y", [(NX, lines, half)], (left, 0), long(got_left))
    got_left = [passed(short(left[by]), "x", by) for by in range(1, NX)]
    right = call(x_to_y_kernel, "right_x", [(NY, lines, half)], (right, 0), *map(long, got_right))
    got_right = passed(short(right[1]), "yh", 1)

    sent = call(
        to_z_kernel, "to_z", [(NZ, 2, rows, panel + 128)],
        (first, 0), long(got_first), (right, 0), long(got_right), (left, 0), *map(long, got_left),
    )
    got = lax.all_to_all(short(sent), "z", 0, 0, tiled=True)
    return call(functools.partial(z_sum_kernel, scale), "z_sum", [(2, rows, panel)], long(got))


def solution(mesh):
    fine = Mesh(mesh.devices.reshape(tuple(SIZES.values())), tuple(SIZES))
    return jax.shard_map(
        per_device,
        mesh=fine,
        in_specs=(P(DP, FACTOR),),
        out_specs=P(None, FACTOR + DP, None),
        check_vma=False,
    )
```

```python
import functools

import jax
import jax.numpy as jnp
from jax import lax
from jax.experimental import pallas as pl
from jax.experimental.pallas import tpu as pltpu
from jax.sharding import Mesh, PartitionSpec as P

SIZES = {"yh": 2, "z": 8, "x": 4, "yl": 2, "core": 2}
DP = ("yh", "z", "x")
FACTOR = ("yl", "core")
NX, NY, NZ = SIZES["x"], SIZES["yh"], SIZES["z"]
NF = SIZES["yl"] * SIZES["core"]
TOP = 15.0
VMEM = 20 * 1024 * 1024
CHUNK = 256


def share(index, count):
    return 1.0 - 0.5 * jnp.float32(index) / count


def lifted(power, factor):
    return jnp.max(jnp.exp2(jnp.full((8, 128), TOP - power))) * factor


def lowered(power, factor):
    return jnp.max(jnp.exp2(jnp.full((8, 128), power - TOP))) / factor


def ahead(axis, by):
    count = SIZES[axis]
    return lax.rem(lax.axis_index(axis) + by + count, count)


def sum_of(terms):
    return functools.reduce(lambda a, b: a + b, terms)


def rows_of(start, count):
    return pl.ds(pl.multiple_of(start, 16), count)


def senders(axis, blocks, growth):
    powers = [jnp.max(block[block.shape[0] - 8 :, :128]) for block in blocks]
    weights = [lowered(p, share(ahead(axis, -by), SIZES[axis])) for by, p in enumerate(powers)]
    return weights, functools.reduce(jnp.maximum, powers) + growth


def products(own_ref, partner_ref, visit):
    tokens, panel = own_ref.shape
    rows = panel // (NX * NY * NZ)
    largest = lambda ref: jnp.max(jnp.abs(ref[...]).astype(jnp.float32))
    bound = tokens * (largest(own_ref) + 1e-15) * (largest(partner_ref) + 1e-15)
    power = jnp.max(jnp.ceil(jnp.log2(jnp.full((8, 128), bound))))
    up = lifted(power, 1.0)
    for c in range(panel // CHUNK):
        product = lax.dot_general(
            own_ref[:, c * CHUNK : (c + 1) * CHUNK], partner_ref[...], (((0,), (0,)), ((), ())),
            preferred_element_type=jnp.float32,
        ) * up
        for n in range(CHUNK // rows):
            yz, x = divmod(c * (CHUNK // rows) + n, NX)
            visit(x, yz // NZ, yz % NZ, product[n * rows : (n + 1) * rows])
    return power


def diagonal_kernel(own_ref, partner_ref, out_ref):
    factor = share(lax.axis_index("x"), NX)

    def visit(x, y, z, value):
        rows = value.shape[0]
        to_x = lax.rem(x - lax.axis_index("x") + NX, NX)
        out_ref[to_x, rows_of((y * NZ + z) * rows, rows), :] = value * factor

    power = products(own_ref, partner_ref, visit)
    out_ref[:, out_ref.shape[1] - 8 :, :] = jnp.full((NX, 8, out_ref.shape[2]), power)


def beside_kernel(own_ref, partner_ref, left_ref, right_ref):
    half = left_ref.shape[2]
    by_y, by_x = share(lax.axis_index("yh"), NY), share(lax.axis_index("x"), NX)

    def visit(x, y, z, value):
        rows = value.shape[0]
        to_x = lax.rem(x - lax.axis_index("x") + NX, NX)
        to_y = lax.rem(y - lax.axis_index("yh") + NY, NY)
        left_ref[to_y, rows_of((to_x * NZ + z) * rows, rows), :] = value[:, :half] * by_y
        right_ref[to_x, rows_of((y * NZ + z) * rows, rows), :] = value[:, half:] * by_x

    power = products(own_ref, partner_ref, visit)
    left_ref[:, left_ref.shape[1] - 8 :, :] = jnp.full((NY, 8, half), power)
    right_ref[:, right_ref.shape[1] - 8 :, :] = jnp.full((NX, 8, half), power)


def x_to_y_kernel(own_ref, *refs):
    out_ref = refs[-1]
    blocks = [own_ref.at[0], *refs[:-1]]
    weights, power = senders("x", blocks, 2.0)
    up = lifted(power, share(lax.axis_index("yh"), NY))
    count = out_ref.shape[1] - 8
    for by in range(NY):
        part = rows_of(ahead("yh", by) * count, count)
        out_ref[by, :count, :] = sum_of([block[part, :] * (w * up) for block, w in zip(blocks, weights)])
    out_ref[:, count:, :] = jnp.full((NY, 8, out_ref.shape[2]), power)


def y_to_x_kernel(own_ref, got_ref, out_ref):
    blocks = [own_ref.at[0], got_ref]
    weights, power = senders("yh", blocks, 1.0)
    up = lifted(power, share(lax.axis_index("x"), NX))
    count = out_ref.shape[1] - 8
    for by in range(NX):
        part = pl.ds(by * count, count)
        out_ref[by, :count, :] = sum_of([block[part, :] * (w * up) for block, w in zip(blocks, weights)])
    out_ref[:, count:, :] = jnp.full((NX, 8, out_ref.shape[2]), power)


def to_z_kernel(*refs):
    first, right, left, out_ref = refs[:NY], refs[NY : 2 * NY], refs[2 * NY : -1], refs[-1]
    first, right, left = ([group[0].at[0], *group[1:]] for group in (first, right, left))
    w_first, p_first = senders("yh", first, 1.0)
    w_right, p_right = senders("yh", right, 1.0)
    w_left, p_left = senders("x", left, 2.0)
    power = jnp.maximum(p_first, jnp.maximum(p_right, p_left))
    up = lifted(power, share(lax.axis_index("z"), NZ))
    _, _, rows, wide = out_ref.shape
    panel = wide - 128
    half = panel // 2
    for z in range(NZ):
        part = pl.ds(z * rows, rows)
        total = lambda blocks, weights: sum_of([block[part, :] * (w * up) for block, w in zip(blocks, weights)])
        out_ref[z, 0, :, :panel] = total(first, w_first)
        out_ref[z, 1, :, :half] = total(left, w_left)
        out_ref[z, 1, :, half:panel] = total(right, w_right)
    out_ref[:, :, :, panel:] = jnp.full((NZ, 2, rows, 128), power)


def z_sum_kernel(scale, got_ref, out_ref):
    panel = out_ref.shape[2]
    for k in range(2):
        weights = [jnp.exp2(got_ref[s, k, :, panel:] - TOP) * (scale / float(1.0 - 0.5 * s / NZ)) for s in range(NZ)]
        for j in range(panel // 128):
            part = slice(j * 128, (j + 1) * 128)
            out_ref[k, :, part] = sum_of([got_ref[s, k, :, part] * w for s, w in enumerate(weights)])


def call(kernel, name, outs, *operands, flops=0):
    whole = lambda shape: pl.BlockSpec(shape, lambda i: (0,) * len(shape))
    arrays = [o[0] if isinstance(o, tuple) else o for o in operands]
    specs = [whole((1, *o[0].shape[1:]) if isinstance(o, tuple) else o.shape) for o in operands]
    out_shape = [jax.ShapeDtypeStruct(shape, jnp.float32) for shape in outs]
    moved = sum(a.size * a.dtype.itemsize for a in arrays) + sum(4 * s.size for s in out_shape)
    result = pl.pallas_call(
        kernel,
        grid=(1,),
        out_shape=out_shape,
        in_specs=specs,
        out_specs=[whole(s.shape) for s in out_shape],
        compiler_params=pltpu.CompilerParams(vmem_limit_bytes=VMEM),
        cost_estimate=pl.CostEstimate(flops=flops, bytes_accessed=moved, transcendentals=0),
        name=name,
    )(*arrays)
    return result if len(outs) > 1 else result[0]


def passed(value, axis, by):
    count = lax.axis_size(axis)
    return lax.ppermute(value, axis, [(i, (i + by) % count) for i in range(count)])


def per_device(acts):
    tokens, panel = acts.shape
    rows = panel // (NX * NY * NZ)
    half = panel // 2
    scale = 1.0 / (tokens * NX * NY * NZ)
    flops = 2 * tokens * panel * panel
    short = lambda value: value.astype(jnp.float16)
    long = lambda value: value.astype(jnp.float32)

    partner = passed(acts, FACTOR, NF - 1)

    first = call(diagonal_kernel, "diagonal", [(NX, NY * NZ * rows + 8, panel)], acts, acts, flops=flops)
    got_first = [passed(short(first[by]), "x", by) for by in range(1, NX)]

    left, right = call(
        beside_kernel, "beside", [(NY, NX * NZ * rows + 8, half), (NX, NY * NZ * rows + 8, half)], acts, partner,
        flops=flops,
    )
    left_sent, right_sent = short(left[1]), [short(right[by]) for by in range(1, NX)]
    got_left = passed(left_sent, "yh", 1)
    got_right = [passed(right_sent[by - 1], "x", by) for by in range(1, NX)]

    ahead_of = [long(jnp.concatenate([s, left_sent[: s.shape[0]]], axis=1)) for s in right_sent]
    got_first = [long(g) + 0.0 * s for g, s in zip(got_first, ahead_of)]

    lines = NZ * rows + 8
    first = call(x_to_y_kernel, "first_x", [(NY, lines, panel)], (first, 0), *got_first)
    got_first = passed(short(first[1]), "yh", 1)
    left = call(y_to_x_kernel, "left_y", [(NX, lines, half)], (left, 0), long(got_left))
    left_sent = [short(left[by]) for by in range(1, NX)]
    got_left = [passed(s, "x", by) for by, s in enumerate(left_sent, 1)]
    ahead_of = [long(jnp.concatenate([s, s], axis=0)[: g.shape[0]]) for s, g in zip(left_sent, got_right)]
    got_right = [long(g) + 0.0 * s for g, s in zip(got_right, ahead_of)]
    right = call(x_to_y_kernel, "right_x", [(NY, lines, half)], (right, 0), *got_right)
    got_right = passed(short(right[1]), "yh", 1)

    sent = call(
        to_z_kernel, "to_z", [(NZ, 2, rows, panel + 128)],
        (first, 0), long(got_first), (right, 0), long(got_right), (left, 0), *map(long, got_left),
    )
    got = lax.all_to_all(short(sent), "z", 0, 0, tiled=True)
    return call(functools.partial(z_sum_kernel, scale), "z_sum", [(2, rows, panel)], long(got))


def solution(mesh):
    fine = Mesh(mesh.devices.reshape(tuple(SIZES.values())), tuple(SIZES))
    return jax.shard_map(
        per_device,
        mesh=fine,
        in_specs=(P(DP, FACTOR),),
        out_specs=P(None, FACTOR + DP, None),
        check_vma=False,
    )
```

```python
import functools

import jax
import jax.numpy as jnp
from jax import lax
from jax.experimental import pallas as pl
from jax.experimental.pallas import tpu as pltpu
from jax.sharding import Mesh, PartitionSpec as P

SIZES = {"yh": 2, "z": 8, "x": 4, "yl": 2, "core": 2}
DP = ("yh", "z", "x")
FACTOR = ("yl", "core")
NX, NY, NZ = SIZES["x"], SIZES["yh"], SIZES["z"]
NF = SIZES["yl"] * SIZES["core"]
TOP = 15.0
VMEM = 20 * 1024 * 1024
CHUNK = 256


def share(index, count):
    return 1.0 - 0.5 * jnp.float32(index) / count


def lifted(power, factor):
    return jnp.max(jnp.exp2(jnp.full((8, 128), TOP - power))) * factor


def lowered(power, factor):
    return jnp.max(jnp.exp2(jnp.full((8, 128), power - TOP))) / factor


def ahead(axis, by):
    count = SIZES[axis]
    return lax.rem(lax.axis_index(axis) + by + count, count)


def sum_of(terms):
    return functools.reduce(lambda a, b: a + b, terms)


def rows_of(start, count):
    return pl.ds(pl.multiple_of(start, 16), count)


def senders(axis, blocks, growth, behind=None):
    powers = [jnp.max(block[block.shape[0] - 8 :, :128]) for block in blocks]
    behind = behind or range(len(blocks))
    weights = [lowered(p, share(ahead(axis, -by), SIZES[axis])) for by, p in zip(behind, powers)]
    return weights, functools.reduce(jnp.maximum, powers) + growth


def products(own_ref, partner_ref, visit):
    tokens, panel = own_ref.shape
    rows = panel // (NX * NY * NZ)
    largest = lambda ref: jnp.max(jnp.abs(ref[...]).astype(jnp.float32))
    bound = tokens * (largest(own_ref) + 1e-15) * (largest(partner_ref) + 1e-15)
    power = jnp.max(jnp.ceil(jnp.log2(jnp.full((8, 128), bound))))
    up = lifted(power, 1.0)
    for c in range(panel // CHUNK):
        product = lax.dot_general(
            own_ref[:, c * CHUNK : (c + 1) * CHUNK], partner_ref[...], (((0,), (0,)), ((), ())),
            preferred_element_type=jnp.float32,
        ) * up
        for n in range(CHUNK // rows):
            yz, x = divmod(c * (CHUNK // rows) + n, NX)
            visit(x, yz // NZ, yz % NZ, product[n * rows : (n + 1) * rows])
    return power


def diagonal_kernel(own_ref, partner_ref, out_ref):
    factor = share(lax.axis_index("x"), NX)

    def visit(x, y, z, value):
        rows = value.shape[0]
        to_x = lax.rem(x - lax.axis_index("x") + NX, NX)
        out_ref[to_x, rows_of((y * NZ + z) * rows, rows), :] = value * factor

    power = products(own_ref, partner_ref, visit)
    out_ref[:, out_ref.shape[1] - 8 :, :] = jnp.full((NX, 8, out_ref.shape[2]), power)


def beside_kernel(own_ref, partner_ref, _, left_ref, right_ref):
    half = left_ref.shape[2]
    by_y, by_x = share(lax.axis_index("yh"), NY), share(lax.axis_index("x"), NX)

    def visit(x, y, z, value):
        rows = value.shape[0]
        to_x = lax.rem(x - lax.axis_index("x") + NX, NX)
        to_y = lax.rem(y - lax.axis_index("yh") + NY, NY)
        left_ref[to_y, rows_of((to_x * NZ + z) * rows, rows), :] = value[:, :half] * by_y
        right_ref[to_x, rows_of((y * NZ + z) * rows, rows), :] = value[:, half:] * by_x

    power = products(own_ref, partner_ref, visit)
    left_ref[:, left_ref.shape[1] - 8 :, :] = jnp.full((NY, 8, half), power)
    right_ref[:, right_ref.shape[1] - 8 :, :] = jnp.full((NX, 8, half), power)


def relay_kernel(next_ref, before_ref, behind_ref, ahead_ref, out_ref):
    count, half = out_ref.shape[1] - 8, out_ref.shape[2] // 2
    (own, behind, beyond), power = senders("x", [next_ref.at[0], behind_ref, ahead_ref], 1.0, (0, 1, NX - 1))
    up = lifted(power, share(lax.axis_index("x"), NX))
    out_ref[0, :count, :half] = next_ref[0, :count, :half] * (own * up) + behind_ref[:count, :] * (behind * up)
    out_ref[0, :count, half:] = next_ref[0, :count, half:] * (own * up)
    out_ref[1, :count, :half] = before_ref[0, :count, :half] * (own * up)
    out_ref[1, :count, half:] = before_ref[0, :count, half:] * (own * up) + ahead_ref[:count, :] * (beyond * up)
    out_ref[:, count:, :] = jnp.full((2, 8, 2 * half), power)


def x_to_y_kernel(behind, own_ref, *refs):
    out_ref = refs[-1]
    blocks = [own_ref.at[0], *refs[:-1]]
    weights, power = senders("x", blocks, 2.0, behind)
    up = lifted(power, share(lax.axis_index("yh"), NY))
    count = out_ref.shape[1] - 8
    for by in range(NY):
        part = rows_of(ahead("yh", by) * count, count)
        out_ref[by, :count, :] = sum_of([block[part, :] * (w * up) for block, w in zip(blocks, weights)])
    out_ref[:, count:, :] = jnp.full((NY, 8, out_ref.shape[2]), power)


def y_to_x_kernel(own_ref, got_ref, out_ref):
    blocks = [own_ref.at[0], got_ref]
    weights, power = senders("yh", blocks, 1.0)
    up = lifted(power, share(lax.axis_index("x"), NX))
    count = out_ref.shape[1] - 8
    for by in range(NX):
        part = pl.ds(by * count, count)
        out_ref[by, :count, :] = sum_of([block[part, :] * (w * up) for block, w in zip(blocks, weights)])
    out_ref[:, count:, :] = jnp.full((NX, 8, out_ref.shape[2]), power)


def to_z_kernel(*refs):
    first, right, left, out_ref = refs[:NY], refs[NY : 2 * NY], refs[2 * NY : -1], refs[-1]
    first, right, left = ([group[0].at[0], *group[1:]] for group in (first, right, left))
    w_first, p_first = senders("yh", first, 1.0)
    w_right, p_right = senders("yh", right, 1.0)
    w_left, p_left = senders("x", left, 2.0)
    power = jnp.maximum(p_first, jnp.maximum(p_right, p_left))
    up = lifted(power, share(lax.axis_index("z"), NZ))
    _, rows, wide = out_ref.shape
    panel = (wide - 128) // 2
    half = panel // 2
    for z in range(NZ):
        part = pl.ds(z * rows, rows)
        total = lambda blocks, weights: sum_of([block[part, :] * (w * up) for block, w in zip(blocks, weights)])
        out_ref[z, :, :panel] = total(first, w_first)
        out_ref[z, :, panel : panel + half] = total(left, w_left)
        out_ref[z, :, panel + half : 2 * panel] = total(right, w_right)
    out_ref[:, :, 2 * panel :] = jnp.full((NZ, rows, 128), power)


def z_sum_kernel(scale, got_ref, out_ref):
    panel = out_ref.shape[2]
    weights = [jnp.exp2(got_ref[s, :, 2 * panel :] - TOP) * (scale / float(1.0 - 0.5 * s / NZ)) for s in range(NZ)]
    for k in range(2):
        for j in range(panel // 128):
            at = k * panel + j * 128
            out_ref[k, :, j * 128 : (j + 1) * 128] = sum_of([got_ref[s, :, at : at + 128] * w for s, w in enumerate(weights)])


def call(kernel, name, outs, *operands, flops=0):
    block = lambda shape, n: pl.BlockSpec(shape, lambda i: (n,) + (0,) * (len(shape) - 1))
    whole = lambda shape: block(shape, 0)
    arrays = [o[0] if isinstance(o, tuple) else o for o in operands]
    specs = [block((1, *o[0].shape[1:]), o[1]) if isinstance(o, tuple) else whole(o.shape) for o in operands]
    out_shape = [jax.ShapeDtypeStruct(shape, jnp.float32) for shape in outs]
    moved = sum(a.size * a.dtype.itemsize for a in arrays) + sum(4 * s.size for s in out_shape)
    result = pl.pallas_call(
        kernel,
        grid=(1,),
        out_shape=out_shape,
        in_specs=specs,
        out_specs=[whole(s.shape) for s in out_shape],
        compiler_params=pltpu.CompilerParams(vmem_limit_bytes=VMEM),
        cost_estimate=pl.CostEstimate(flops=flops, bytes_accessed=moved, transcendentals=0),
        name=name,
    )(*arrays)
    return result if len(outs) > 1 else result[0]


def passed(value, axis, by):
    count = lax.axis_size(axis)
    return lax.ppermute(value, axis, [(i, (i + by) % count) for i in range(count)])


def per_device(acts):
    tokens, panel = acts.shape
    rows = panel // (NX * NY * NZ)
    half = panel // 2
    scale = 1.0 / (tokens * NX * NY * NZ)
    flops = 2 * tokens * panel * panel
    short = lambda value: value.astype(jnp.float16)
    long = lambda value: value.astype(jnp.float32)

    partner = passed(acts, FACTOR, NF - 1)

    first = call(diagonal_kernel, "diagonal", [(NX, NY * NZ * rows + 8, panel)], acts, acts, flops=flops)
    behind = long(passed(short(first[2, :, :half]), "x", 1))
    beyond = long(passed(short(first[2, :, half:]), "x", NX - 1))
    relay = call(relay_kernel, "relay", [(2, NY * NZ * rows + 8, panel)], (first, 1), (first, 3), behind, beyond)
    got_first = [passed(short(relay[0]), "x", 1), passed(short(relay[1]), "x", NX - 1)]

    left, right = call(
        beside_kernel, "beside", [(NY, NX * NZ * rows + 8, half), (NX, NY * NZ * rows + 8, half)], acts, partner,
        (relay, 0), flops=flops,
    )
    left_sent, right_sent = short(left[1]), [short(right[by]) for by in range(1, NX)]
    got_left = passed(left_sent, "yh", 1)
    got_right = [passed(right_sent[by - 1], "x", by) for by in range(1, NX)]

    ahead_of = [long(jnp.concatenate([s, left_sent[: s.shape[0]]], axis=1)) for s in right_sent]
    got_first = [long(g) + 0.0 * s for g, s in zip(got_first, ahead_of)]

    lines = NZ * rows + 8
    over_two = functools.partial(x_to_y_kernel, (0, 1, NX - 1))
    over_all = functools.partial(x_to_y_kernel, None)
    first = call(over_two, "first_x", [(NY, lines, panel)], (first, 0), *got_first)
    got_first = passed(short(first[1]), "yh", 1)
    left = call(y_to_x_kernel, "left_y", [(NX, lines, half)], (left, 0), long(got_left))
    left_sent = [short(left[by]) for by in range(1, NX)]
    got_left = [passed(s, "x", by) for by, s in enumerate(left_sent, 1)]
    ahead_of = [long(jnp.concatenate([s, s], axis=0)[: g.shape[0]]) for s, g in zip(left_sent, got_right)]
    got_right = [long(g) + 0.0 * s for g, s in zip(got_right, ahead_of)]
    right = call(over_all, "right_x", [(NY, lines, half)], (right, 0), *got_right)
    got_right = passed(short(right[1]), "yh", 1)

    sent = call(
        to_z_kernel, "to_z", [(NZ, rows, 2 * panel + 128)],
        (first, 0), long(got_first), (right, 0), long(got_right), (left, 0), *map(long, got_left),
    )
    got = lax.all_to_all(short(sent), "z", 0, 0, tiled=True)
    return call(functools.partial(z_sum_kernel, scale), "z_sum", [(2, rows, panel)], long(got))


def solution(mesh):
    fine = Mesh(mesh.devices.reshape(tuple(SIZES.values())), tuple(SIZES))
    return jax.shard_map(
        per_device,
        mesh=fine,
        in_specs=(P(DP, FACTOR),),
        out_specs=P(None, FACTOR + DP, None),
        check_vma=False,
    )
```

```python
import functools

import jax
import jax.numpy as jnp
from jax import lax
from jax.experimental import pallas as pl
from jax.experimental.pallas import tpu as pltpu
from jax.sharding import Mesh, PartitionSpec as P

SIZES = {"yh": 2, "z": 8, "x": 4, "yl": 2, "core": 2}
DP = ("yh", "z", "x")
FACTOR = ("yl", "core")
NX, NY, NZ = SIZES["x"], SIZES["yh"], SIZES["z"]
NF = SIZES["yl"] * SIZES["core"]
TOP = 15.0
VMEM = 20 * 1024 * 1024
CHUNK = 256


def share(index, count):
    return 1.0 - 0.5 * jnp.float32(index) / count


def lifted(power, factor):
    return jnp.max(jnp.exp2(jnp.full((8, 128), TOP - power))) * factor


def lowered(power, factor):
    return jnp.max(jnp.exp2(jnp.full((8, 128), power - TOP))) / factor


def ahead(axis, by):
    count = SIZES[axis]
    return lax.rem(lax.axis_index(axis) + by + count, count)


def sum_of(terms):
    return functools.reduce(lambda a, b: a + b, terms)


def rows_of(start, count):
    return pl.ds(pl.multiple_of(start, 16), count)


def senders(axis, blocks, growth, behind=None):
    powers = [jnp.max(block[block.shape[0] - 8 :, :128]) for block in blocks]
    behind = behind or range(len(blocks))
    weights = [lowered(p, share(ahead(axis, -by), SIZES[axis])) for by, p in zip(behind, powers)]
    return weights, functools.reduce(jnp.maximum, powers) + growth


def products(own_ref, partner_ref, visit):
    tokens, panel = own_ref.shape
    rows = panel // (NX * NY * NZ)
    largest = lambda ref: jnp.max(jnp.abs(ref[...]).astype(jnp.float32))
    bound = tokens * (largest(own_ref) + 1e-15) * (largest(partner_ref) + 1e-15)
    power = jnp.max(jnp.ceil(jnp.log2(jnp.full((8, 128), bound))))
    up = lifted(power, 1.0)
    for c in range(panel // CHUNK):
        product = lax.dot_general(
            own_ref[:, c * CHUNK : (c + 1) * CHUNK], partner_ref[...], (((0,), (0,)), ((), ())),
            preferred_element_type=jnp.float32,
        ) * up
        for n in range(CHUNK // rows):
            yz, x = divmod(c * (CHUNK // rows) + n, NX)
            visit(x, yz // NZ, yz % NZ, product[n * rows : (n + 1) * rows])
    return power


def diagonal_kernel(own_ref, partner_ref, out_ref):
    factor = share(lax.axis_index("x"), NX)

    def visit(x, y, z, value):
        rows = value.shape[0]
        to_x = lax.rem(x - lax.axis_index("x") + NX, NX)
        out_ref[to_x, rows_of((y * NZ + z) * rows, rows), :] = value * factor

    power = products(own_ref, partner_ref, visit)
    out_ref[:, out_ref.shape[1] - 8 :, :] = jnp.full((NX, 8, out_ref.shape[2]), power)


def beside_kernel(own_ref, partner_ref, _, left_ref, right_ref):
    half = left_ref.shape[2]
    by_y, by_x = share(lax.axis_index("yh"), NY), share(lax.axis_index("x"), NX)

    def visit(x, y, z, value):
        rows = value.shape[0]
        to_x = lax.rem(x - lax.axis_index("x") + NX, NX)
        to_y = lax.rem(y - lax.axis_index("yh") + NY, NY)
        left_ref[to_y, rows_of((to_x * NZ + z) * rows, rows), :] = value[:, :half] * by_y
        part, middle = rows_of((y * NZ + z) * rows, rows), right_ref.shape[2] // 2
        slot = jnp.where(to_x == 0, 0, lax.rem(to_x + 1, NX - 1) + 1)
        right_ref[slot, part, :middle] = value[:, half : half + middle] * by_x
        right_ref[to_x, part, middle:] = value[:, half + middle :] * by_x

    power = products(own_ref, partner_ref, visit)
    left_ref[:, left_ref.shape[1] - 8 :, :] = jnp.full((NY, 8, half), power)
    right_ref[:, right_ref.shape[1] - 8 :, :] = jnp.full((NX, 8, half), power)


def relay_kernel(next_ref, before_ref, behind_ref, ahead_ref, out_ref):
    count, half = out_ref.shape[1] - 8, out_ref.shape[2] // 2
    (own, behind, beyond), power = senders("x", [next_ref.at[0], behind_ref, ahead_ref], 1.0, (0, 1, NX - 1))
    up = lifted(power, share(lax.axis_index("x"), NX))
    out_ref[0, :count, :half] = next_ref[0, :count, :half] * (own * up) + behind_ref[:count, :] * (behind * up)
    out_ref[0, :count, half:] = next_ref[0, :count, half:] * (own * up)
    out_ref[1, :count, :half] = before_ref[0, :count, :half] * (own * up)
    out_ref[1, :count, half:] = before_ref[0, :count, half:] * (own * up) + ahead_ref[:count, :] * (beyond * up)
    out_ref[:, count:, :] = jnp.full((2, 8, 2 * half), power)


def join_kernel(joins_ref, behind_ref, ahead_ref, out_ref):
    count, half = out_ref.shape[1] - 8, out_ref.shape[2]
    (own, behind, beyond), power = senders("x", [joins_ref.at[0], behind_ref, ahead_ref], 1.0, (0, 1, NX - 1))
    up = lifted(power, share(lax.axis_index("x"), NX))
    out_ref[0, :count, :] = joins_ref[0, :count, :half] * (own * up) + behind_ref[:count, :half] * (behind * up)
    out_ref[1, :count, :] = joins_ref[0, :count, half:] * (own * up) + ahead_ref[:count, half:] * (beyond * up)
    out_ref[:, count:, :] = jnp.full((2, 8, half), power)


def joined_to_y_kernel(own_ref, behind_ref, ahead_ref, from_behind_ref, from_ahead_ref, out_ref):
    count, half = out_ref.shape[1] - 8, out_ref.shape[2] // 2
    blocks = [own_ref.at[0], behind_ref, ahead_ref, from_behind_ref, from_ahead_ref]
    weights, power = senders("x", blocks, 2.0, (0, 1, NX - 1, 1, NX - 1))
    up = lifted(power, share(lax.axis_index("yh"), NY))
    own, behind, beyond, from_behind, from_ahead = (w * up for w in weights)
    for by in range(NY):
        part = rows_of(ahead("yh", by) * count, count)
        out_ref[by, :count, :half] = (
            own_ref[0, part, :half] * own + ahead_ref[part, :half] * beyond + from_behind_ref[part, :] * from_behind
        )
        out_ref[by, :count, half:] = (
            own_ref[0, part, half:] * own + behind_ref[part, half:] * behind + from_ahead_ref[part, :] * from_ahead
        )
    out_ref[:, count:, :] = jnp.full((NY, 8, 2 * half), power)


def x_to_y_kernel(behind, own_ref, *refs):
    out_ref = refs[-1]
    blocks = [own_ref.at[0], *refs[:-1]]
    weights, power = senders("x", blocks, 2.0, behind)
    up = lifted(power, share(lax.axis_index("yh"), NY))
    count = out_ref.shape[1] - 8
    for by in range(NY):
        part = rows_of(ahead("yh", by) * count, count)
        out_ref[by, :count, :] = sum_of([block[part, :] * (w * up) for block, w in zip(blocks, weights)])
    out_ref[:, count:, :] = jnp.full((NY, 8, out_ref.shape[2]), power)


def y_to_x_kernel(own_ref, got_ref, out_ref):
    blocks = [own_ref.at[0], got_ref]
    weights, power = senders("yh", blocks, 1.0)
    up = lifted(power, share(lax.axis_index("x"), NX))
    count = out_ref.shape[1] - 8
    for by in range(NX):
        part = pl.ds(by * count, count)
        out_ref[by, :count, :] = sum_of([block[part, :] * (w * up) for block, w in zip(blocks, weights)])
    out_ref[:, count:, :] = jnp.full((NX, 8, out_ref.shape[2]), power)


def to_z_kernel(*refs):
    first, right, left, out_ref = refs[:NY], refs[NY : 2 * NY], refs[2 * NY : -1], refs[-1]
    first, right, left = ([group[0].at[0], *group[1:]] for group in (first, right, left))
    w_first, p_first = senders("yh", first, 1.0)
    w_right, p_right = senders("yh", right, 1.0)
    w_left, p_left = senders("x", left, 2.0)
    power = jnp.maximum(p_first, jnp.maximum(p_right, p_left))
    up = lifted(power, share(lax.axis_index("z"), NZ))
    _, rows, wide = out_ref.shape
    panel = (wide - 128) // 2
    half = panel // 2
    for z in range(NZ):
        part = pl.ds(z * rows, rows)
        total = lambda blocks, weights: sum_of([block[part, :] * (w * up) for block, w in zip(blocks, weights)])
        out_ref[z, :, :panel] = total(first, w_first)
        out_ref[z, :, panel : panel + half] = total(left, w_left)
        out_ref[z, :, panel + half : 2 * panel] = total(right, w_right)
    out_ref[:, :, 2 * panel :] = jnp.full((NZ, rows, 128), power)


def z_sum_kernel(scale, got_ref, out_ref):
    panel = out_ref.shape[2]
    weights = [jnp.exp2(got_ref[s, :, 2 * panel :] - TOP) * (scale / float(1.0 - 0.5 * s / NZ)) for s in range(NZ)]
    for k in range(2):
        for j in range(panel // 128):
            at = k * panel + j * 128
            out_ref[k, :, j * 128 : (j + 1) * 128] = sum_of([got_ref[s, :, at : at + 128] * w for s, w in enumerate(weights)])


def call(kernel, name, outs, *operands, flops=0):
    block = lambda shape, n: pl.BlockSpec(shape, lambda i: (n,) + (0,) * (len(shape) - 1))
    whole = lambda shape: block(shape, 0)
    arrays = [o[0] if isinstance(o, tuple) else o for o in operands]
    specs = [block((1, *o[0].shape[1:]), o[1]) if isinstance(o, tuple) else whole(o.shape) for o in operands]
    out_shape = [jax.ShapeDtypeStruct(shape, jnp.float32) for shape in outs]
    moved = sum(a.size * a.dtype.itemsize for a in arrays) + sum(4 * s.size for s in out_shape)
    result = pl.pallas_call(
        kernel,
        grid=(1,),
        out_shape=out_shape,
        in_specs=specs,
        out_specs=[whole(s.shape) for s in out_shape],
        compiler_params=pltpu.CompilerParams(vmem_limit_bytes=VMEM),
        cost_estimate=pl.CostEstimate(flops=flops, bytes_accessed=moved, transcendentals=0),
        name=name,
    )(*arrays)
    return result if len(outs) > 1 else result[0]


def passed(value, axis, by):
    count = lax.axis_size(axis)
    return lax.ppermute(value, axis, [(i, (i + by) % count) for i in range(count)])


def per_device(acts):
    tokens, panel = acts.shape
    rows = panel // (NX * NY * NZ)
    half = panel // 2
    scale = 1.0 / (tokens * NX * NY * NZ)
    flops = 2 * tokens * panel * panel
    short = lambda value: value.astype(jnp.float16)
    long = lambda value: value.astype(jnp.float32)

    partner = passed(acts, FACTOR, NF - 1)

    first = call(diagonal_kernel, "diagonal", [(NX, NY * NZ * rows + 8, panel)], acts, acts, flops=flops)
    behind = long(passed(short(first[2, :, :half]), "x", 1))
    beyond = long(passed(short(first[2, :, half:]), "x", NX - 1))
    relay = call(relay_kernel, "relay", [(2, NY * NZ * rows + 8, panel)], (first, 1), (first, 3), behind, beyond)
    got_first = [passed(short(relay[0]), "x", 1), passed(short(relay[1]), "x", NX - 1)]

    left, right = call(
        beside_kernel, "beside", [(NY, NX * NZ * rows + 8, half), (NX, NY * NZ * rows + 8, half)], acts, partner,
        (relay, 0), flops=flops,
    )
    quarter = half // 2
    left_sent, right_sent = short(left[1]), [short(right[1]), short(right[2])]
    got_left = passed(left_sent, "yh", 1)
    behind, beyond = long(passed(right_sent[0], "x", 1)), long(passed(right_sent[1], "x", NX - 1))

    ahead_of = long(jnp.concatenate([right_sent[1], left_sent[: right_sent[1].shape[0]]], axis=1))
    got_first = [long(g) + 0.0 * ahead_of for g in got_first]
    relay = call(join_kernel, "join", [(2, NY * NZ * rows + 8, quarter)], (right, 3), behind, beyond)
    got_right = [passed(short(relay[0]), "x", 1), passed(short(relay[1]), "x", NX - 1)]

    lines = NZ * rows + 8
    over_two = functools.partial(x_to_y_kernel, (0, 1, NX - 1))
    first = call(over_two, "first_x", [(NY, lines, panel)], (first, 0), *got_first)
    got_first = passed(short(first[1]), "yh", 1)
    left = call(y_to_x_kernel, "left_y", [(NX, lines, half)], (left, 0), long(got_left))
    left_sent = [short(left[by]) for by in range(1, NX)]
    got_left = [passed(s, "x", by) for by, s in enumerate(left_sent, 1)]
    tied = [long(jnp.concatenate([s, s], axis=0)[: g.shape[0], :quarter]) for s, g in zip(left_sent, got_right)]
    got_right = [long(g) + 0.0 * s for g, s in zip(got_right, tied)]
    right = call(joined_to_y_kernel, "right_x", [(NY, lines, half)], (right, 0), behind, beyond, *got_right)
    got_right = passed(short(right[1]), "yh", 1)

    sent = call(
        to_z_kernel, "to_z", [(NZ, rows, 2 * panel + 128)],
        (first, 0), long(got_first), (right, 0), long(got_right), (left, 0), *map(long, got_left),
    )
    got = lax.all_to_all(short(sent), "z", 0, 0, tiled=True)
    return call(functools.partial(z_sum_kernel, scale), "z_sum", [(2, rows, panel)], long(got))


def solution(mesh):
    fine = Mesh(mesh.devices.reshape(tuple(SIZES.values())), tuple(SIZES))
    return jax.shard_map(
        per_device,
        mesh=fine,
        in_specs=(P(DP, FACTOR),),
        out_specs=P(None, FACTOR + DP, None),
        check_vma=False,
    )
```

```python
import functools

import jax
import jax.numpy as jnp
from jax import lax
from jax.experimental import pallas as pl
from jax.experimental.pallas import tpu as pltpu
from jax.sharding import Mesh, PartitionSpec as P

SIZES = {"yh": 2, "z": 8, "x": 4, "yl": 2, "core": 2}
DP = ("yh", "z", "x")
FACTOR = ("yl", "core")
NX, NY, NZ = SIZES["x"], SIZES["yh"], SIZES["z"]
NF = SIZES["yl"] * SIZES["core"]
TOP = 15.0
VMEM = 20 * 1024 * 1024
CHUNK = 256


def share(index, count):
    return 1.0 - 0.5 * jnp.float32(index) / count


def lifted(power, factor):
    return jnp.max(jnp.exp2(jnp.full((8, 128), TOP - power))) * factor


def lowered(power, factor):
    return jnp.max(jnp.exp2(jnp.full((8, 128), power - TOP))) / factor


def ahead(axis, by):
    count = SIZES[axis]
    return lax.rem(lax.axis_index(axis) + by + count, count)


def sum_of(terms):
    return functools.reduce(lambda a, b: a + b, terms)


def rows_of(start, count):
    return pl.ds(pl.multiple_of(start, 16), count)


def senders(axis, blocks, growth, behind=None):
    powers = [jnp.max(block[block.shape[0] - 8 :, :128]) for block in blocks]
    behind = behind or range(len(blocks))
    weights = [lowered(p, share(ahead(axis, -by), SIZES[axis])) for by, p in zip(behind, powers)]
    return weights, functools.reduce(jnp.maximum, powers) + growth


def products(own_ref, partner_ref, visit):
    tokens, panel = own_ref.shape
    rows = panel // (NX * NY * NZ)
    largest = lambda ref: jnp.max(jnp.abs(ref[...]).astype(jnp.float32))
    bound = tokens * (largest(own_ref) + 1e-15) * (largest(partner_ref) + 1e-15)
    power = jnp.max(jnp.ceil(jnp.log2(jnp.full((8, 128), bound))))
    up = lifted(power, 1.0)
    for c in range(panel // CHUNK):
        product = lax.dot_general(
            own_ref[:, c * CHUNK : (c + 1) * CHUNK], partner_ref[...], (((0,), (0,)), ((), ())),
            preferred_element_type=jnp.float32,
        ) * up
        for n in range(CHUNK // rows):
            yz, x = divmod(c * (CHUNK // rows) + n, NX)
            visit(x, yz // NZ, yz % NZ, product[n * rows : (n + 1) * rows])
    return power


def diagonal_kernel(own_ref, partner_ref, out_ref):
    factor = share(lax.axis_index("x"), NX)

    def visit(x, y, z, value):
        rows = value.shape[0]
        to_x = lax.rem(x - lax.axis_index("x") + NX, NX)
        out_ref[to_x, rows_of((y * NZ + z) * rows, rows), :] = value * factor

    power = products(own_ref, partner_ref, visit)
    out_ref[:, out_ref.shape[1] - 8 :, :] = jnp.full((NX, 8, out_ref.shape[2]), power)


def beside_kernel(own_ref, partner_ref, _, left_ref, right_ref):
    half = left_ref.shape[2]
    by_y, by_x = share(lax.axis_index("yh"), NY), share(lax.axis_index("x"), NX)

    def visit(x, y, z, value):
        rows = value.shape[0]
        to_x = lax.rem(x - lax.axis_index("x") + NX, NX)
        to_y = lax.rem(y - lax.axis_index("yh") + NY, NY)
        left_ref[to_y, rows_of((to_x * NZ + z) * rows, rows), :] = value[:, :half] * by_y
        part, middle = rows_of((y * NZ + z) * rows, rows), right_ref.shape[2] // 2
        slot = jnp.where(to_x == 0, 0, lax.rem(to_x + 1, NX - 1) + 1)
        right_ref[slot, part, :middle] = value[:, half : half + middle] * by_x
        right_ref[to_x, part, middle:] = value[:, half + middle :] * by_x

    power = products(own_ref, partner_ref, visit)
    left_ref[:, left_ref.shape[1] - 8 :, :] = jnp.full((NY, 8, half), power)
    right_ref[:, right_ref.shape[1] - 8 :, :] = jnp.full((NX, 8, half), power)


def relay_kernel(next_ref, before_ref, behind_ref, ahead_ref, out_ref):
    count, half = out_ref.shape[1] - 8, out_ref.shape[2] // 2
    (own, behind, beyond), power = senders("x", [next_ref.at[0], behind_ref, ahead_ref], 1.0, (0, 1, NX - 1))
    up = lifted(power, share(lax.axis_index("x"), NX))
    out_ref[0, :count, :half] = next_ref[0, :count, :half] * (own * up) + behind_ref[:count, :] * (behind * up)
    out_ref[0, :count, half:] = next_ref[0, :count, half:] * (own * up)
    out_ref[1, :count, :half] = before_ref[0, :count, :half] * (own * up)
    out_ref[1, :count, half:] = before_ref[0, :count, half:] * (own * up) + ahead_ref[:count, :] * (beyond * up)
    out_ref[:, count:, :] = jnp.full((2, 8, 2 * half), power)


def join_kernel(joins_ref, behind_ref, ahead_ref, out_ref):
    count, half = out_ref.shape[1] - 8, out_ref.shape[2]
    (own, behind, beyond), power = senders("x", [joins_ref.at[0], behind_ref, ahead_ref], 1.0, (0, 1, NX - 1))
    up = lifted(power, share(lax.axis_index("x"), NX))
    out_ref[0, :count, :] = joins_ref[0, :count, :half] * (own * up) + behind_ref[:count, :half] * (behind * up)
    out_ref[1, :count, :] = joins_ref[0, :count, half:] * (own * up) + ahead_ref[:count, half:] * (beyond * up)
    out_ref[:, count:, :] = jnp.full((2, 8, half), power)


def joined_to_y_kernel(own_ref, behind_ref, ahead_ref, from_behind_ref, from_ahead_ref, out_ref):
    count, half = out_ref.shape[1] - 8, out_ref.shape[2] // 2
    blocks = [own_ref.at[0], behind_ref, ahead_ref, from_behind_ref, from_ahead_ref]
    weights, power = senders("x", blocks, 2.0, (0, 1, NX - 1, 1, NX - 1))
    up = lifted(power, share(lax.axis_index("yh"), NY))
    own, behind, beyond, from_behind, from_ahead = (w * up for w in weights)
    for by in range(NY):
        part = rows_of(ahead("yh", by) * count, count)
        out_ref[by, :count, :half] = (
            own_ref[0, part, :half] * own + ahead_ref[part, :half] * beyond + from_behind_ref[part, :] * from_behind
        )
        out_ref[by, :count, half:] = (
            own_ref[0, part, half:] * own + behind_ref[part, half:] * behind + from_ahead_ref[part, :] * from_ahead
        )
    out_ref[:, count:, :] = jnp.full((NY, 8, 2 * half), power)


def x_to_y_kernel(behind, own_ref, *refs):
    out_ref = refs[-1]
    blocks = [own_ref.at[0], *refs[:-1]]
    weights, power = senders("x", blocks, 2.0, behind)
    up = lifted(power, share(lax.axis_index("yh"), NY))
    count = out_ref.shape[1] - 8
    for by in range(NY):
        part = rows_of(ahead("yh", by) * count, count)
        out_ref[by, :count, :] = sum_of([block[part, :] * (w * up) for block, w in zip(blocks, weights)])
    out_ref[:, count:, :] = jnp.full((NY, 8, out_ref.shape[2]), power)


def y_to_x_kernel(own_ref, got_ref, out_ref):
    blocks = [own_ref.at[0], got_ref]
    weights, power = senders("yh", blocks, 1.0)
    up = lifted(power, share(lax.axis_index("x"), NX))
    count = out_ref.shape[1] - 8
    for by in range(NX):
        part = pl.ds(by * count, count)
        out_ref[by, :count, :] = sum_of([block[part, :] * (w * up) for block, w in zip(blocks, weights)])
    out_ref[:, count:, :] = jnp.full((NX, 8, out_ref.shape[2]), power)


def to_z_kernel(*refs):
    first, right, left, out_ref = refs[:NY], refs[NY : 2 * NY], refs[2 * NY : -1], refs[-1]
    first, right, left = ([group[0].at[0], *group[1:]] for group in (first, right, left))
    w_first, p_first = senders("yh", first, 1.0)
    w_right, p_right = senders("yh", right, 1.0)
    w_left, p_left = senders("x", left, 2.0)
    power = jnp.maximum(p_first, jnp.maximum(p_right, p_left))
    up = lifted(power, share(lax.axis_index("z"), NZ))
    _, rows, wide = out_ref.shape
    panel = (wide - 128) // 2
    half = panel // 2
    for z in range(NZ):
        part = pl.ds(z * rows, rows)
        total = lambda blocks, weights: sum_of([block[part, :] * (w * up) for block, w in zip(blocks, weights)])
        out_ref[z, :, :panel] = total(first, w_first)
        out_ref[z, :, panel : panel + half] = total(left, w_left)
        out_ref[z, :, panel + half : 2 * panel] = total(right, w_right)
    out_ref[:, :, 2 * panel :] = jnp.full((NZ, rows, 128), power)


def z_sum_kernel(scale, got_ref, out_ref):
    panel = out_ref.shape[2]
    weights = [jnp.exp2(got_ref[s, :, 2 * panel :] - TOP) * (scale / float(1.0 - 0.5 * s / NZ)) for s in range(NZ)]
    for k in range(2):
        for j in range(panel // 128):
            at = k * panel + j * 128
            out_ref[k, :, j * 128 : (j + 1) * 128] = sum_of([got_ref[s, :, at : at + 128] * w for s, w in enumerate(weights)])


def call(kernel, name, outs, *operands, flops=0):
    block = lambda shape, n: pl.BlockSpec(shape, lambda i: (n,) + (0,) * (len(shape) - 1))
    whole = lambda shape: block(shape, 0)
    arrays = [o[0] if isinstance(o, tuple) else o for o in operands]
    specs = [block((1, *o[0].shape[1:]), o[1]) if isinstance(o, tuple) else whole(o.shape) for o in operands]
    out_shape = [jax.ShapeDtypeStruct(shape, jnp.float32) for shape in outs]
    moved = sum(a.size * a.dtype.itemsize for a in arrays) + sum(4 * s.size for s in out_shape)
    result = pl.pallas_call(
        kernel,
        grid=(1,),
        out_shape=out_shape,
        in_specs=specs,
        out_specs=[whole(s.shape) for s in out_shape],
        compiler_params=pltpu.CompilerParams(vmem_limit_bytes=VMEM),
        cost_estimate=pl.CostEstimate(flops=flops, bytes_accessed=moved, transcendentals=0),
        name=name,
    )(*arrays)
    return result if len(outs) > 1 else result[0]


def passed(value, axis, by):
    count = lax.axis_size(axis)
    return lax.ppermute(value, axis, [(i, (i + by) % count) for i in range(count)])


def per_device(acts):
    tokens, panel = acts.shape
    rows = panel // (NX * NY * NZ)
    half = panel // 2
    scale = 1.0 / (tokens * NX * NY * NZ)
    flops = 2 * tokens * panel * panel
    short = lambda value: value.astype(jnp.float16)
    long = lambda value: value.astype(jnp.float32)

    partner = passed(acts, FACTOR, NF - 1)

    first = call(diagonal_kernel, "diagonal", [(NX, NY * NZ * rows + 8, panel)], acts, acts, flops=flops)
    behind = long(passed(short(first[2, :, :half]), "x", 1))
    beyond = long(passed(short(first[2, :, half:]), "x", NX - 1))
    relay = call(relay_kernel, "relay", [(2, NY * NZ * rows + 8, panel)], (first, 1), (first, 3), behind, beyond)
    got_first = [passed(short(relay[0]), "x", 1), passed(short(relay[1]), "x", NX - 1)]

    left, right = call(
        beside_kernel, "beside", [(NY, NX * NZ * rows + 8, half), (NX, NY * NZ * rows + 8, half)], acts, partner,
        (relay, 0), flops=flops,
    )
    quarter = half // 2
    left_sent, right_sent = short(left[1]), [short(right[1]), short(right[2])]
    got_left = passed(left_sent, "yh", 1)
    behind, beyond = long(passed(right_sent[0], "x", 1)), long(passed(right_sent[1], "x", NX - 1))

    relay = call(join_kernel, "join", [(2, NY * NZ * rows + 8, quarter)], (right, 3), behind, beyond)
    joined_sent = [short(relay[0]), short(relay[1])]
    got_right = [passed(joined_sent[0], "x", 1), passed(joined_sent[1], "x", NX - 1)]

    ahead_of = long(jnp.concatenate([*joined_sent, left_sent[: relay.shape[1]]], axis=1))
    got_first = [long(g) + 0.0 * ahead_of for g in got_first]

    lines = NZ * rows + 8
    over_two = functools.partial(x_to_y_kernel, (0, 1, NX - 1))
    first = call(over_two, "first_x", [(NY, lines, panel)], (first, 0), *got_first)
    got_first = passed(short(first[1]), "yh", 1)
    left = call(y_to_x_kernel, "left_y", [(NX, lines, half)], (left, 0), long(got_left))
    left_sent = [short(left[by]) for by in range(1, NX)]
    got_left = [passed(s, "x", by) for by, s in enumerate(left_sent, 1)]
    tied = [long(jnp.concatenate([s, s], axis=0)[: g.shape[0], :quarter]) for s, g in zip(left_sent, got_right)]
    got_right = [long(g) + 0.0 * s for g, s in zip(got_right, tied)]
    right = call(joined_to_y_kernel, "right_x", [(NY, lines, half)], (right, 0), behind, beyond, *got_right)
    got_right = passed(short(right[1]), "yh", 1)

    sent = call(
        to_z_kernel, "to_z", [(NZ, rows, 2 * panel + 128)],
        (first, 0), long(got_first), (right, 0), long(got_right), (left, 0), *map(long, got_left),
    )
    got = lax.all_to_all(short(sent), "z", 0, 0, tiled=True)
    return call(functools.partial(z_sum_kernel, scale), "z_sum", [(2, rows, panel)], long(got))


def solution(mesh):
    fine = Mesh(mesh.devices.reshape(tuple(SIZES.values())), tuple(SIZES))
    return jax.shard_map(
        per_device,
        mesh=fine,
        in_specs=(P(DP, FACTOR),),
        out_specs=P(None, FACTOR + DP, None),
        check_vma=False,
    )
```
